256 devices in a mesh: seq: 64 (over x, z, core), head: 4 (over y).
Axes of the slice: x: 4, y: 4, z: 8, core: 2. Of those that a mesh axis runs over, the one named last changes fastest.
Arguments:
- query: bfloat16 [32768, 5120], P(('seq', 'head')), may hold values from -6 to 6
- key: bfloat16 [32768, 5120], P(('seq', 'head')), may hold values from -6 to 6
- value: bfloat16 [32768, 5120], P(('seq', 'head')), may hold values from -6 to 6
- grad_out: bfloat16 [32768, 5120], P(('seq', 'head')), may hold values from -6 to 6
- lengths: int32 [128], replicated, may hold values from 1 to 512, 32768 in all
Outputs:
- attended: bfloat16 [32768, 5120], P(('seq', 'head'))
- grad_query: bfloat16 [32768, 5120], P(('seq', 'head'))
- grad_key: bfloat16 [32768, 5120], P(('seq', 'head'))
- grad_value: bfloat16 [32768, 5120], P(('seq', 'head'))
The draws below stay inside these ranges and needn't reach their ends.
All inputs are finite; a program needn't handle non-finite values.
Results may differ from the reference program's by a relative error of at most 0.012.
The reference program's roundings to bfloat16 on the way (of `probs_low` and `dscores`) count: a program that leaves them out, or rounds other values in their place, can miss the bound.
Values may be sent and summed in bfloat16 or wider, within the bound.
No kernel may reach another device: no remote copies, remote signals or barrier semaphores. Data moves between devices by JAX's collectives and lax.ppermute only.
A program may use at most 128 MiB of HBM per device.

```python
import math
import jax
import jax.numpy as jnp
import numpy as np
from jax import lax

D = 5120
HEADS = 40
HEAD_DIM = 128
SEQ_BLOCK = 512
TOKENS = 32768
PROTEINS = 128


def draw_query(key, part):
    key = jax.random.fold_in(key, 1)
    return jnp.clip(jax.random.normal(key, (TOKENS, D), jnp.float32), -6.0, 6.0).astype(jnp.bfloat16)


def draw_key(key, part):
    key = jax.random.fold_in(key, 2)
    return jnp.clip(jax.random.normal(key, (TOKENS, D), jnp.float32), -6.0, 6.0).astype(jnp.bfloat16)


def block_levels(rng, dims, pieces, least, top_value):
    loudness = 1.0
    for dim, blocks in pieces:
        draws = jax.random.uniform(jax.random.fold_in(jax.random.fold_in(rng, 6), dim), (blocks,), jnp.float32, least / len(pieces), top_value / len(pieces))
        loudness = loudness * jnp.repeat(jnp.exp(draws), dims[dim] // blocks).reshape((-1,) + (1,) * (len(dims) - 1 - dim))
    return loudness


def length_profile(number_of, total, most, skew):
    portions = [(1 << 20) // math.isqrt(grade ** skew) + 1 for grade in range(2, number_of + 1)]
    surplus, given = total - most - (number_of - 1), [1] * (number_of - 1)
    while surplus > 0:
        free = [i for i in range(number_of - 1) if given[i] < most]
        pool, budget = sum([portions[i] for i in free]), surplus
        for i in free:
            more = min(most - given[i], max(1, budget * portions[i] // pool), surplus)
            given[i] = given[i] + more
            surplus = surplus - more
    return np.array([most] + given)


def uneven(rng, number_of, total, bound, slope):
    if number_of == 2:
        one = jax.random.randint(rng, (), max(1, total - bound), min(bound, total - 1) + 1)
        return jnp.stack([one, total - one])
    sizes = jnp.asarray(length_profile(number_of, total, bound, slope), jnp.int32)
    couples = (number_of - 1) // 2
    source_of, receiver = sizes[1:1 + 2 * couples:2], sizes[2:2 + 2 * couples:2]
    room = jnp.minimum(source_of - 1, bound - receiver)
    shifted = jax.random.randint(jax.random.fold_in(rng, 1), (couples,), 0, 1 << 20) % (room + 1)
    sizes = sizes.at[1:1 + 2 * couples:2].set(source_of - shifted).at[2:2 + 2 * couples:2].set(receiver + shifted)
    return sizes[jax.random.permutation(jax.random.fold_in(rng, 2), number_of)]


def normal_values(stream_key, dims, width, reach, cuts=(), kind=jnp.bfloat16):
    level = block_levels(stream_key, dims, cuts, -0.22, 0.18) if cuts else 1.0
    values = jax.random.normal(stream_key, dims, jnp.float32) * width * level
    return jnp.minimum(jnp.maximum(values, -reach), reach).astype(kind)


def setup_inputs(seed: int = 0) -> dict:
    splits = jax.random.split(jax.random.key(seed), 6)
    query = draw_query(jax.random.fold_in(splits[5], 71), 0)
    key = draw_key(jax.random.fold_in(splits[5], 71), 0)
    value = normal_values(splits[2], (TOKENS, D), 1.0, 6.0, ((0, 256),))
    grad_out = normal_values(splits[3], (TOKENS, D), 1.0, 6.0, ((0, 256),))
    lengths = uneven(splits[4], PROTEINS, TOKENS, SEQ_BLOCK, 2).astype(jnp.int32)
    return {"query": query, "key": key, "value": value, "grad_out": grad_out, "lengths": lengths}


NEG_FILL = -1e30


def protein_ids(lengths, positions, total_len):
    ends = jnp.cumsum(lengths, dtype=jnp.int32)
    counted = jnp.sum((ends[None, :] <= positions[:, None]).astype(jnp.int32), axis=1)
    inside = (positions >= 0) & (positions < total_len)
    return jnp.where(inside, counted, -1).astype(jnp.int32)


def reference(query, key, value, grad_out, lengths):
    block = SEQ_BLOCK
    blocks = TOKENS // SEQ_BLOCK
    positions = jnp.arange(TOKENS + 2 * block, dtype=jnp.int32) - block
    owners = protein_ids(lengths, positions, TOKENS)
    own_ids = owners[block:block + TOKENS].reshape(blocks, block)
    win_index = (jnp.arange(blocks, dtype=jnp.int32)[:, None] * block + jnp.arange(3 * block, dtype=jnp.int32)[None, :]).astype(jnp.int32)
    win_ids = owners[win_index]
    allowed = own_ids[:, :, None] == win_ids[:, None, :]
    score_scale = 1.0 / (HEAD_DIM ** 0.5)

    def windows(column):
        empty = jnp.zeros((block, HEAD_DIM), column.dtype)
        padded = jnp.concatenate((empty, column, empty), axis=0)
        below = padded[:TOKENS].reshape(blocks, block, HEAD_DIM)
        middle = padded[block:block + TOKENS].reshape(blocks, block, HEAD_DIM)
        above = padded[2 * block:2 * block + TOKENS].reshape(blocks, block, HEAD_DIM)
        return jnp.concatenate((below, middle, above), axis=1)

    def one_head(operands):
        query_h, key_h, value_h, grad_h = operands
        query_c = query_h.reshape(blocks, block, HEAD_DIM).astype(jnp.float32)
        grad_c = grad_h.reshape(blocks, block, HEAD_DIM).astype(jnp.float32)
        key_w = windows(key_h).astype(jnp.float32)
        value_w = windows(value_h).astype(jnp.float32)
        scores = jnp.einsum("cqd,ckd->cqk", query_c, key_w) * score_scale
        scores = jnp.where(allowed, scores, NEG_FILL)
        row_max = jnp.max(scores, axis=2, keepdims=True)
        row_sum = jnp.sum(jnp.exp(scores - row_max), axis=2, keepdims=True)
        log_total = row_max + jnp.log(row_sum)
        probs = jnp.exp(scores - log_total)
        probs_low = lax.optimization_barrier(probs.astype(jnp.bfloat16)).astype(jnp.float32)
        attended = jnp.einsum("cqk,ckd->cqd", probs_low, value_w).astype(jnp.bfloat16)
        row_delta = jnp.sum(grad_c * attended.astype(jnp.float32), axis=2, keepdims=True)
        dprobs = jnp.einsum("cqd,ckd->cqk", grad_c, value_w)
        dscores = lax.optimization_barrier((probs * (dprobs - row_delta) * score_scale).astype(jnp.bfloat16)).astype(jnp.float32)
        grad_q = jnp.einsum("cqk,ckd->cqd", dscores, key_w).astype(jnp.bfloat16)
        grad_kw = jnp.einsum("cqk,cqd->ckd", dscores, query_c)
        grad_vw = jnp.einsum("cqk,cqd->ckd", probs_low, grad_c)
        zero_block = jnp.zeros((1, block, HEAD_DIM), jnp.float32)

        def assemble(terms):
            middle = terms[:, block:2 * block]
            from_above = jnp.concatenate((terms[1:, :block], zero_block), axis=0)
            from_below = jnp.concatenate((zero_block, terms[:-1, 2 * block:]), axis=0)
            return (middle + from_above + from_below).astype(jnp.bfloat16).reshape(TOKENS, HEAD_DIM)

        return (attended.reshape(TOKENS, HEAD_DIM), grad_q.reshape(TOKENS, HEAD_DIM), assemble(grad_kw), assemble(grad_vw))

    def heads_first(array):
        return array.reshape(TOKENS, HEADS, HEAD_DIM).transpose(1, 0, 2)

    def heads_back(array):
        return array.transpose(1, 0, 2).reshape(TOKENS, HEADS * HEAD_DIM)

    results = lax.map(one_head, (heads_first(query), heads_first(key), heads_first(value), heads_first(grad_out)))
    return (heads_back(results[0]), heads_back(results[1]), heads_back(results[2]), heads_back(results[3]))
```

```python
import math

import jax
import jax.numpy as jnp
from jax import lax
from jax.experimental import pallas as pl
from jax.experimental.pallas import tpu as pltpu
from jax.sharding import PartitionSpec as P

HEAD_DIM = 128
HALF = 256
ROWS = 128
NEG_FILL = -1e30
LOG2E = math.log2(math.e)

PIECES = (2, 2, 2, 2, 2)

GROUP = 2
SPANS = (3, 5, 8)

ORDER = (
    "P0", "P1", "P2", "A0", "A1", "P3", "K0", "A2", "P4",
    "K1", "A3", "K2", "M0", "A4", "K3", "M1", "U0", "K4",
    "M2", "U1", "M3", "U2", "M4", "U3", "U4",
)

PAIR_FLOPS = 6 * 2 * HALF * HALF * HEAD_DIM
PAIRS = 14


def cost(n_bytes, flops=0):
    return pl.CostEstimate(flops=flops, bytes_accessed=n_bytes, transcendentals=0)


VMEM_LIMIT = 24 * 1024 * 1024
PACK_LIMIT = 60 * 1024 * 1024

ANY = pl.BlockSpec(memory_space=pl.ANY)
HBM = pl.BlockSpec(memory_space=pltpu.HBM)
VMEM = pl.BlockSpec(memory_space=pltpu.VMEM)


def perm_head(x, k):
    return lax.ppermute(x, "head", [(i, (i + k) % 4) for i in range(4)])


def shifted(x, steps):
    n = lax.axis_size("seq")
    return lax.ppermute(x, "seq", [(i, (i + steps) % n) for i in range(n)])


def run_copies(copies):
    for copy in copies:
        copy.start()
    for copy in copies:
        copy.wait()


def call_dma(body, ins, tok, outs, n_sems, in_spec, out_spec, aliases=None, limit=None):
    toks = [] if tok is None else [tok]

    def kernel(*refs):
        n = len(ins)
        body(refs[:n], refs[n + len(toks) : -1], refs[-1])

    return pl.pallas_call(
        kernel,
        in_specs=in_spec + [ANY] * len(toks),
        out_specs=[out_spec] * len(outs),
        out_shape=outs,
        scratch_shapes=[pltpu.SemaphoreType.DMA((n_sems,))],
        input_output_aliases=aliases or {},
        cost_estimate=cost(1 << 20 ),
        compiler_params=pltpu.CompilerParams(vmem_limit_bytes=limit or VMEM_LIMIT),
    )(*ins, *toks)


def bf(*shape):
    return jax.ShapeDtypeStruct(shape, jnp.bfloat16)


def pack(arrays, off, w, per_dev, tok):
    def body(ins, outs, sems):
        y = lax.axis_index("head")
        copies = []
        for k in (2, 1, 3, 0):
            col = pl.multiple_of(lax.rem(y + k, 4) * per_dev + off, HEAD_DIM)
            for a in range(4):
                copies.append(
                    pltpu.make_async_copy(
                        ins[a].at[:, pl.ds(col, w)], outs[k].at[a], sems.at[len(copies)]
                    )
                )
        run_copies(copies)

    return call_dma(body, arrays, tok, [bf(4, ROWS, w)] * 4, 16, [HBM] * 4, VMEM,
                    limit=PACK_LIMIT)


def assemble_kernel(p0, p1, p2, p3, _, out):
    y = lax.axis_index("head")
    for k, part in enumerate((p0, p1, p2, p3)):
        row = pl.multiple_of(lax.rem(y + 4 - k, 4) * ROWS, ROWS)
        out[:, pl.ds(row, ROWS), :] = part[...]


def assemble(parts, w, tok):
    return pl.pallas_call(
        assemble_kernel,
        in_specs=[VMEM] * 4 + [ANY],
        out_specs=VMEM,
        out_shape=bf(4, 4 * ROWS, w),
        cost_estimate=cost(1 << 20 ),
        compiler_params=pltpu.CompilerParams(vmem_limit_bytes=VMEM_LIMIT),
    )(*parts, tok)


def unpack(parts, dest, off, w, per_dev, width, tok):
    first = dest is None
    dest = [] if first else list(dest)

    def body(ins, outs, sems):
        y = lax.axis_index("head")
        copies = []
        for k in range(4):
            col = pl.multiple_of(lax.rem(y + 4 - k, 4) * per_dev + off, HEAD_DIM)
            for a in range(4):
                copies.append(
                    pltpu.make_async_copy(
                        ins[k].at[a], outs[a].at[:, pl.ds(col, w)], sems.at[len(copies)]
                    )
                )
        run_copies(copies)

    return call_dma(
        body,
        [*parts, *dest],
        tok,
        [bf(ROWS, width)] * 4 + [bf(16, HEAD_DIM)],
        16,
        [VMEM] * 4 + [HBM] * len(dest),
        HBM,
        aliases={} if first else {4 + a: a for a in range(4)},
    )


def mm(a, b):
    return jnp.dot(a, b, preferred_element_type=jnp.float32)


def attention_kernel(
    first, kind, ours, above, id_row, id_col, _, own, up, *scratch
):
    k_all, v_all, q_t, k_t, v_t, g_t, att_t, gq_t, acc_k, acc_v = scratch
    scale = 1.0 / math.sqrt(HEAD_DIM)
    group = k_all.shape[0]
    lower, upper = slice(0, 2 * HALF), slice(2 * HALF, 4 * HALF)
    lanes = [slice(h * HEAD_DIM, (h + 1) * HEAD_DIM) for h in range(group)]
    for h in range(group):
        for span, tile in ((lower, ours), (upper, above)):
            k_all[h, span, :] = tile[1, :, lanes[h]]
            v_all[h, span, :] = tile[2, :, lanes[h]]
            for a, out in enumerate((q_t, k_t, v_t, g_t)):
                out[h, :, span] = tile[a, :, lanes[h]].T
    acc_k[...] = jnp.zeros_like(acc_k)
    acc_v[...] = jnp.zeros_like(acc_v)

    def tile_work(i, n):
        size = n * ROWS
        cols = pl.ds(pl.multiple_of(i * HALF, HALF), HALF)
        keys = pl.ds(pl.multiple_of(first[i] * ROWS, ROWS), size)
        hs = range(group)
        idk = id_col[keys, :]
        ok = jnp.concatenate([idk, idk], axis=1) == id_row[:1, cols]
        qt = [q_t[h, :, cols] for h in hs]
        gt = [g_t[h, :, cols] for h in hs]
        s = [mm(k_all[h, keys, :], qt[h]) for h in hs]
        p, low = [], []
        for h in hs:
            x = jnp.where(ok, s[h] * (scale * LOG2E), NEG_FILL)
            top = jnp.maximum(x.max(axis=0, keepdims=True), 0.1 * NEG_FILL)
            e = jnp.exp2(x - top)
            inv = 1.0 / jnp.maximum(e.sum(axis=0, keepdims=True), 1e-30)
            p.append(e * inv)
            low.append(p[h].astype(jnp.bfloat16))
        dp = [mm(v_all[h, keys, :], gt[h]) for h in hs]
        att = [mm(v_t[h, :, keys], low[h]).astype(jnp.bfloat16) for h in hs]
        gv = [mm(low[h], gt[h].T) for h in hs]
        ds = []
        for h in hs:
            delta = jnp.sum(
                gt[h].astype(jnp.float32) * att[h].astype(jnp.float32), axis=0, keepdims=True
            )
            ds.append((p[h] * (dp[h] - delta) * scale).astype(jnp.bfloat16))
        gq = [mm(k_t[h, :, keys], ds[h]).astype(jnp.bfloat16) for h in hs]
        gk = [mm(ds[h], qt[h].T) for h in hs]
        for h in hs:
            att_t[h, :, cols] = att[h]
            gq_t[h, :, cols] = gq[h]
            acc_k[h, keys, :] += gk[h]
            acc_v[h, keys, :] += gv[h]

    def one(i, carry):
        for m, n in enumerate(SPANS):
            pl.when(kind[i] == m)(lambda n=n: tile_work(i, n))
        return carry

    lax.fori_loop(0, 4, one, 0)
    for h in range(group):
        for a, t in ((0, att_t), (1, gq_t)):
            x = t[h].T
            own[a, :, lanes[h]] = x[lower, :]
            up[a, :, lanes[h]] = x[upper, :]
        for a, acc in ((2, acc_k), (3, acc_v)):
            own[a, :, lanes[h]] = acc[h, lower, :].astype(jnp.bfloat16)
            up[a, :, lanes[h]] = acc[h, upper, :].astype(jnp.bfloat16)


def attention(own, above, places, heads, tok):
    first, kind, id_row, id_col = places
    w = heads * HEAD_DIM
    group = GROUP if heads % GROUP == 0 else 1
    rows = 4 * HALF
    wide = pl.BlockSpec((4, 2 * HALF, group * HEAD_DIM), lambda h: (0, 0, h))
    smem = pl.BlockSpec(memory_space=pltpu.SMEM)
    return pl.pallas_call(
        attention_kernel,
        grid=(heads // group,),
        in_specs=[smem] * 2
        + [wide] * 2
        + [
            pl.BlockSpec(id_row.shape, lambda h: (0, 0)),
            pl.BlockSpec(id_col.shape, lambda h: (0, 0)),
            ANY,
        ],
        out_specs=[wide, wide],
        out_shape=[bf(4, 2 * HALF, w)] * 2,
        scratch_shapes=[pltpu.VMEM((group, rows, HEAD_DIM), jnp.bfloat16)] * 2
        + [pltpu.VMEM((group, HEAD_DIM, rows), jnp.bfloat16)] * 6
        + [pltpu.VMEM((group, rows, HEAD_DIM), jnp.float32)] * 2,
        cost_estimate=cost(heads * 32 * HALF * HEAD_DIM * 2, heads * PAIRS * PAIR_FLOPS),
        compiler_params=pltpu.CompilerParams(vmem_limit_bytes=VMEM_LIMIT),
    )(first, kind, own, above, id_row, id_col, tok)


def merge_kernel(own, below, foreign, _, s0, s1, s2, s3):
    y = lax.axis_index("head")
    for k, out in enumerate((s0, s1, s2, s3)):
        rows = pl.ds(pl.multiple_of(lax.rem(y + k, 4) * ROWS, ROWS), ROWS)
        theirs = foreign[rows, :1] != 0
        for a in range(4):
            x = own[a, rows, :].astype(jnp.float32)
            z = below[a, rows, :].astype(jnp.float32)
            out[a] = jnp.where(theirs, z, x).astype(jnp.bfloat16)


def merge(own, below, foreign, w, tok):
    return pl.pallas_call(
        merge_kernel,
        in_specs=[VMEM] * 3 + [ANY],
        out_specs=[VMEM] * 4,
        out_shape=[bf(4, ROWS, w)] * 4,
        cost_estimate=cost(1 << 20 ),
        compiler_params=pltpu.CompilerParams(vmem_limit_bytes=VMEM_LIMIT),
    )(own, below, foreign, tok)


def protein_places(lengths, block):
    ends = jnp.cumsum(lengths, dtype=jnp.int32)[None, :]
    start = lax.axis_index("seq") * block
    stop = start + block
    total = block * lax.axis_size("seq")
    pos = start + jnp.arange(2 * block, dtype=jnp.int32)
    past = ends <= pos[:, None]
    ids = jnp.sum(past.astype(jnp.int32), axis=1)
    begin = jnp.max(jnp.where(past, ends, 0), axis=1)
    end = jnp.min(jnp.where(past, total, ends), axis=1)
    ours = (pos < total) & (begin >= start) & (begin < stop)

    tiles = (-1, HALF)
    lo = jnp.min(jnp.where(ours, begin, start + 4 * HALF).reshape(tiles), axis=1) - start
    hi = jnp.max(jnp.where(ours, end, start).reshape(tiles), axis=1) - start
    first = lo // ROWS
    count = (hi + ROWS - 1) // ROWS - first
    kind = sum((count > n).astype(jnp.int32) for n in SPANS[:-1])
    sizes = SPANS[0] + sum(
        (kind > m) * (SPANS[m + 1] - SPANS[m]) for m in range(len(SPANS) - 1)
    )
    first = jnp.clip(first, 0, 4 * HALF // ROWS - sizes)
    kind = jnp.where(count > 0, kind, -1)

    id_row = jnp.broadcast_to(jnp.where(ours, ids, -1)[None, :], (8, ids.shape[0]))
    id_col = jnp.broadcast_to(jnp.where(ours, ids, -2)[:, None], (ids.shape[0], HEAD_DIM))
    foreign = 1 - ours[:block].astype(jnp.int32)
    foreign = jnp.broadcast_to(foreign[:, None], (block, HEAD_DIM))
    return (first, kind, id_row, id_col), foreign


def shards(query, key, value, grad_out, lengths):
    arrays = (query, key, value, grad_out)
    width = query.shape[1]
    per_dev = width // 4
    block = 2 * HALF
    places, foreign = protein_places(lengths, block)
    offs = [sum(PIECES[:c]) * HEAD_DIM for c in range(len(PIECES))]
    widths = [n * HEAD_DIM for n in PIECES]
    got, whole, above, result, ready = {}, {}, {}, {}, {}
    dest = None
    tok = None
    for step in ORDER:
        op, c = step[0], int(step[1:])
        w, off = widths[c], offs[c]
        if op == "P":
            sent = pack(arrays, off, w, per_dev, tok)
            got[c] = [sent[0]] + [perm_head(sent[k], k) for k in (1, 2, 3)]
            tok = sent[0]
        elif op == "A":
            tok = whole[c] = assemble(got[c], w, tok)
            above[c] = shifted(whole[c], -1)
        elif op == "K":
            own, up = attention(whole[c], above[c], places, PIECES[c], tok)
            result[c] = (own, shifted(up, 1))
            tok = own
        elif op == "M":
            parts = merge(*result[c], foreign, w, tok)
            ready[c] = [parts[0]] + [perm_head(parts[k], k) for k in (1, 2, 3)]
            tok = parts[0]
        else:
            *dest, tok = unpack(ready[c], dest, off, w, per_dev, width, tok)
    return tuple(dest)


def solution(mesh):
    rows = P(("seq", "head"), None)
    return jax.shard_map(
        shards,
        mesh=mesh,
        in_specs=(rows, rows, rows, rows, P()),
        out_specs=(rows, rows, rows, rows),
        check_vma=False,
    )
```

```python
import math

import jax
import jax.numpy as jnp
from jax import lax
from jax.experimental import pallas as pl
from jax.experimental.pallas import tpu as pltpu
from jax.sharding import PartitionSpec as P

HEAD_DIM = 128
HALF = 256
ROWS = 128
NEG_FILL = -1e30
LOG2E = math.log2(math.e)

PIECES = (2, 2, 2, 2, 2)

GROUP = 2
SPANS = (3, 5, 8)

ORDER = (
    "P0", "P1", "P2", "P3", "A0", "A1", "P4", "K0", "A2",
    "K1", "A3", "K2", "M0", "A4", "K3", "M1", "U0", "K4",
    "M2", "U1", "M3", "U2", "M4", "U3", "U4",
)

PAIR_FLOPS = 6 * 2 * HALF * HALF * HEAD_DIM
PAIRS = 14


def cost(n_bytes, flops=0):
    return pl.CostEstimate(flops=flops, bytes_accessed=n_bytes, transcendentals=0)


VMEM_LIMIT = 24 * 1024 * 1024
PACK_LIMIT = 60 * 1024 * 1024

ANY = pl.BlockSpec(memory_space=pl.ANY)
HBM = pl.BlockSpec(memory_space=pltpu.HBM)
VMEM = pl.BlockSpec(memory_space=pltpu.VMEM)


def perm_head(x, k):
    return lax.ppermute(x, "head", [(i, (i + k) % 4) for i in range(4)])


def shifted(x, steps):
    n = lax.axis_size("seq")
    return lax.ppermute(x, "seq", [(i, (i + steps) % n) for i in range(n)])


def run_copies(copies):
    for copy in copies:
        copy.start()
    for copy in copies:
        copy.wait()


def call_dma(body, ins, tok, outs, n_sems, in_spec, out_spec, aliases=None, limit=None):
    toks = [] if tok is None else [tok]

    def kernel(*refs):
        n = len(ins)
        body(refs[:n], refs[n + len(toks) : -1], refs[-1])

    return pl.pallas_call(
        kernel,
        in_specs=in_spec + [ANY] * len(toks),
        out_specs=[out_spec] * len(outs),
        out_shape=outs,
        scratch_shapes=[pltpu.SemaphoreType.DMA((n_sems,))],
        input_output_aliases=aliases or {},
        cost_estimate=cost(1 << 20 ),
        compiler_params=pltpu.CompilerParams(vmem_limit_bytes=limit or VMEM_LIMIT),
    )(*ins, *toks)


def bf(*shape):
    return jax.ShapeDtypeStruct(shape, jnp.bfloat16)


def pack(arrays, off, w, per_dev, tok):
    def body(ins, outs, sems):
        y = lax.axis_index("head")
        copies = []
        for k in (2, 1, 3, 0):
            col = pl.multiple_of(lax.rem(y + k, 4) * per_dev + off, HEAD_DIM)
            for a in range(4):
                copies.append(
                    pltpu.make_async_copy(
                        ins[a].at[:, pl.ds(col, w)], outs[k].at[a], sems.at[len(copies)]
                    )
                )
        run_copies(copies)

    return call_dma(body, arrays, tok, [bf(4, ROWS, w)] * 4, 16, [HBM] * 4, VMEM,
                    limit=PACK_LIMIT)


def assemble_kernel(p0, p1, p2, p3, _, out):
    y = lax.axis_index("head")
    for k, part in enumerate((p0, p1, p2, p3)):
        row = pl.multiple_of(lax.rem(y + 4 - k, 4) * ROWS, ROWS)
        out[:, pl.ds(row, ROWS), :] = part[...]


def assemble(parts, w, tok):
    return pl.pallas_call(
        assemble_kernel,
        in_specs=[VMEM] * 4 + [ANY],
        out_specs=VMEM,
        out_shape=bf(4, 4 * ROWS, w),
        cost_estimate=cost(1 << 20 ),
        compiler_params=pltpu.CompilerParams(vmem_limit_bytes=VMEM_LIMIT),
    )(*parts, tok)


def unpack(parts, dest, off, w, per_dev, width, tok):
    first = dest is None
    dest = [] if first else list(dest)

    def body(ins, outs, sems):
        y = lax.axis_index("head")
        copies = []
        for k in range(4):
            col = pl.multiple_of(lax.rem(y + 4 - k, 4) * per_dev + off, HEAD_DIM)
            for a in range(4):
                copies.append(
                    pltpu.make_async_copy(
                        ins[k].at[a], outs[a].at[:, pl.ds(col, w)], sems.at[len(copies)]
                    )
                )
        run_copies(copies)

    return call_dma(
        body,
        [*parts, *dest],
        tok,
        [bf(ROWS, width)] * 4 + [bf(16, HEAD_DIM)],
        16,
        [VMEM] * 4 + [HBM] * len(dest),
        HBM,
        aliases={} if first else {4 + a: a for a in range(4)},
    )


def mm(a, b):
    return jnp.dot(a, b, preferred_element_type=jnp.float32)


def attention_kernel(
    first, kind, ours, above, id_row, id_col, _, own, up, *scratch
):
    k_all, v_all, q_t, k_t, v_t, g_t, att_t, gq_t, acc_k, acc_v = scratch
    scale = 1.0 / math.sqrt(HEAD_DIM)
    group = k_all.shape[0]
    lower, upper = slice(0, 2 * HALF), slice(2 * HALF, 4 * HALF)
    lanes = [slice(h * HEAD_DIM, (h + 1) * HEAD_DIM) for h in range(group)]
    for h in range(group):
        for span, tile in ((lower, ours), (upper, above)):
            k_all[h, span, :] = tile[1, :, lanes[h]]
            v_all[h, span, :] = tile[2, :, lanes[h]]
            for a, out in enumerate((q_t, k_t, v_t, g_t)):
                out[h, :, span] = tile[a, :, lanes[h]].T
    acc_k[...] = jnp.zeros_like(acc_k)
    acc_v[...] = jnp.zeros_like(acc_v)

    def tile_work(i, n):
        size = n * ROWS
        cols = pl.ds(pl.multiple_of(i * HALF, HALF), HALF)
        keys = pl.ds(pl.multiple_of(first[i] * ROWS, ROWS), size)
        hs = range(group)
        idk = id_col[keys, :]
        ok = jnp.concatenate([idk, idk], axis=1) == id_row[:1, cols]
        qt = [q_t[h, :, cols] for h in hs]
        gt = [g_t[h, :, cols] for h in hs]
        s = [mm(k_all[h, keys, :], qt[h]) for h in hs]
        p, low = [], []
        for h in hs:
            x = jnp.where(ok, s[h] * (scale * LOG2E), NEG_FILL)
            top = jnp.maximum(x.max(axis=0, keepdims=True), 0.1 * NEG_FILL)
            e = jnp.exp2(x - top)
            inv = 1.0 / jnp.maximum(e.sum(axis=0, keepdims=True), 1e-30)
            p.append(e * inv)
            low.append(p[h].astype(jnp.bfloat16))
        dp = [mm(v_all[h, keys, :], gt[h]) for h in hs]
        att = [mm(v_t[h, :, keys], low[h]).astype(jnp.bfloat16) for h in hs]
        gv = [mm(low[h], gt[h].T) for h in hs]
        ds = []
        for h in hs:
            delta = jnp.sum(
                gt[h].astype(jnp.float32) * att[h].astype(jnp.float32), axis=0, keepdims=True
            )
            ds.append((p[h] * (dp[h] - delta) * scale).astype(jnp.bfloat16))
        gq = [mm(k_t[h, :, keys], ds[h]).astype(jnp.bfloat16) for h in hs]
        gk = [mm(ds[h], qt[h].T) for h in hs]
        for h in hs:
            att_t[h, :, cols] = att[h]
            gq_t[h, :, cols] = gq[h]
            acc_k[h, keys, :] += gk[h]
            acc_v[h, keys, :] += gv[h]

    def one(i, carry):
        for m, n in enumerate(SPANS):
            pl.when(kind[i] == m)(lambda n=n: tile_work(i, n))
        return carry

    lax.fori_loop(0, 4, one, 0)
    for h in range(group):
        for a, t in ((0, att_t), (1, gq_t)):
            x = t[h].T
            own[a, :, lanes[h]] = x[lower, :]
            up[a, :, lanes[h]] = x[upper, :]
        for a, acc in ((2, acc_k), (3, acc_v)):
            own[a, :, lanes[h]] = acc[h, lower, :].astype(jnp.bfloat16)
            up[a, :, lanes[h]] = acc[h, upper, :].astype(jnp.bfloat16)


def attention(own, above, places, heads, tok):
    first, kind, id_row, id_col = places
    w = heads * HEAD_DIM
    group = GROUP if heads % GROUP == 0 else 1
    rows = 4 * HALF
    wide = pl.BlockSpec((4, 2 * HALF, group * HEAD_DIM), lambda h: (0, 0, h))
    smem = pl.BlockSpec(memory_space=pltpu.SMEM)
    return pl.pallas_call(
        attention_kernel,
        grid=(heads // group,),
        in_specs=[smem] * 2
        + [wide] * 2
        + [
            pl.BlockSpec(id_row.shape, lambda h: (0, 0)),
            pl.BlockSpec(id_col.shape, lambda h: (0, 0)),
            ANY,
        ],
        out_specs=[wide, wide],
        out_shape=[bf(4, 2 * HALF, w)] * 2,
        scratch_shapes=[pltpu.VMEM((group, rows, HEAD_DIM), jnp.bfloat16)] * 2
        + [pltpu.VMEM((group, HEAD_DIM, rows), jnp.bfloat16)] * 6
        + [pltpu.VMEM((group, rows, HEAD_DIM), jnp.float32)] * 2,
        cost_estimate=cost(heads * 32 * HALF * HEAD_DIM * 2, heads * PAIRS * PAIR_FLOPS),
        compiler_params=pltpu.CompilerParams(vmem_limit_bytes=VMEM_LIMIT),
    )(first, kind, own, above, id_row, id_col, tok)


def merge_kernel(own, below, foreign, _, s0, s1, s2, s3):
    y = lax.axis_index("head")
    for k, out in enumerate((s0, s1, s2, s3)):
        rows = pl.ds(pl.multiple_of(lax.rem(y + k, 4) * ROWS, ROWS), ROWS)
        theirs = foreign[rows, :1] != 0
        for a in range(4):
            x = own[a, rows, :].astype(jnp.float32)
            z = below[a, rows, :].astype(jnp.float32)
            out[a] = jnp.where(theirs, z, x).astype(jnp.bfloat16)


def merge(own, below, foreign, w, tok):
    return pl.pallas_call(
        merge_kernel,
        in_specs=[VMEM] * 3 + [ANY],
        out_specs=[VMEM] * 4,
        out_shape=[bf(4, ROWS, w)] * 4,
        cost_estimate=cost(1 << 20 ),
        compiler_params=pltpu.CompilerParams(vmem_limit_bytes=VMEM_LIMIT),
    )(own, below, foreign, tok)


def protein_places(lengths, block):
    ends = jnp.cumsum(lengths, dtype=jnp.int32)[None, :]
    start = lax.axis_index("seq") * block
    stop = start + block
    total = block * lax.axis_size("seq")
    pos = start + jnp.arange(2 * block, dtype=jnp.int32)
    past = ends <= pos[:, None]
    ids = jnp.sum(past.astype(jnp.int32), axis=1)
    begin = jnp.max(jnp.where(past, ends, 0), axis=1)
    end = jnp.min(jnp.where(past, total, ends), axis=1)
    ours = (pos < total) & (begin >= start) & (begin < stop)

    tiles = (-1, HALF)
    lo = jnp.min(jnp.where(ours, begin, start + 4 * HALF).reshape(tiles), axis=1) - start
    hi = jnp.max(jnp.where(ours, end, start).reshape(tiles), axis=1) - start
    first = lo // ROWS
    count = (hi + ROWS - 1) // ROWS - first
    kind = sum((count > n).astype(jnp.int32) for n in SPANS[:-1])
    sizes = SPANS[0] + sum(
        (kind > m) * (SPANS[m + 1] - SPANS[m]) for m in range(len(SPANS) - 1)
    )
    first = jnp.clip(first, 0, 4 * HALF // ROWS - sizes)
    kind = jnp.where(count > 0, kind, -1)

    id_row = jnp.broadcast_to(jnp.where(ours, ids, -1)[None, :], (8, ids.shape[0]))
    id_col = jnp.broadcast_to(jnp.where(ours, ids, -2)[:, None], (ids.shape[0], HEAD_DIM))
    foreign = 1 - ours[:block].astype(jnp.int32)
    foreign = jnp.broadcast_to(foreign[:, None], (block, HEAD_DIM))
    return (first, kind, id_row, id_col), foreign


def shards(query, key, value, grad_out, lengths):
    arrays = (query, key, value, grad_out)
    width = query.shape[1]
    per_dev = width // 4
    block = 2 * HALF
    places, foreign = protein_places(lengths, block)
    offs = [sum(PIECES[:c]) * HEAD_DIM for c in range(len(PIECES))]
    widths = [n * HEAD_DIM for n in PIECES]
    got, whole, above, result, ready = {}, {}, {}, {}, {}
    dest = None
    tok = None
    for step in ORDER:
        op, c = step[0], int(step[1:])
        w, off = widths[c], offs[c]
        if op == "P":
            sent = pack(arrays, off, w, per_dev, tok)
            got[c] = [sent[0]] + [perm_head(sent[k], k) for k in (1, 2, 3)]
            tok = sent[0]
        elif op == "A":
            tok = whole[c] = assemble(got[c], w, tok)
            above[c] = shifted(whole[c], -1)
        elif op == "K":
            own, up = attention(whole[c], above[c], places, PIECES[c], tok)
            result[c] = (own, shifted(up, 1))
            tok = own
        elif op == "M":
            parts = merge(*result[c], foreign, w, tok)
            ready[c] = [parts[0]] + [perm_head(parts[k], k) for k in (1, 2, 3)]
            tok = parts[0]
        else:
            *dest, tok = unpack(ready[c], dest, off, w, per_dev, width, tok)
    return tuple(dest)


def solution(mesh):
    rows = P(("seq", "head"), None)
    return jax.shard_map(
        shards,
        mesh=mesh,
        in_specs=(rows, rows, rows, rows, P()),
        out_specs=(rows, rows, rows, rows),
        check_vma=False,
    )
```
